512 devices in a mesh: row: 16 (over z_lo, core), col: 32 (over y, x, z_hi).
Axes of the slice: x: 4, y: 4, z: 16 (z_hi: 2, z_lo: 8; z = z_hi * 8 + z_lo), core: 2. Of those that a mesh axis runs over, the one named last changes fastest.
Arguments:
- tokens: bfloat16 [1280, 12288], P('col', 'row'), may hold values from -6 to 6
- inner_weight: bfloat16 [12288, 24576], P('row', 'col'), may hold values from -0.0546875 to 0.0546875
- inner_bias: bfloat16 [24576], P('col'), may hold values from -3 to 3
- outer_weight: bfloat16 [24576, 12288], P('col', 'row'), may hold values from -0.0390625 to 0.0390625
- outer_bias: bfloat16 [12288], P('row'), may hold values from -3 to 3
Outputs:
- block_output: bfloat16 [1280, 12288], P('col', 'row')
The draws below stay inside these ranges and needn't reach their ends.
All inputs are finite; a program needn't handle non-finite values.
Results may differ from the reference program's by a relative error of at most 0.028.
Values may be sent and summed in bfloat16 or wider, within the bound.
No kernel may reach another device: no remote copies, remote signals or barrier semaphores. Data moves between devices by JAX's collectives and lax.ppermute only.
A program may use at most 64 MiB of HBM per device.

```python
import jax
import jax.numpy as jnp
from jax import lax

D = 12288
FF = 24576
TOKENS = 1280
N_ROW = 16
N_COL = 32


def levels(own_key, shape, cuts, low, top_value):
    factor_of, own = 1.0, jax.random.fold_in(own_key, 6)
    for dim, blocks in cuts:
        steps = jnp.exp(jax.random.uniform(jax.random.fold_in(own, dim), (blocks,), jnp.float32, low / len(cuts), top_value / len(cuts)))
        factor_of = factor_of * jnp.repeat(steps, shape[dim] // blocks).reshape([-1 if axis == dim else 1 for axis in range(len(shape))])
    return factor_of


def centred(key, shape, scale, reach, pieces=(), kind=jnp.bfloat16):
    level = levels(key, shape, pieces, -0.22, 0.18) if pieces else 1.0
    values = jax.random.normal(key, shape, jnp.float32) * scale * level
    return jnp.minimum(jnp.maximum(values, -reach), reach).astype(kind)


def setup_inputs(seed: int = 0) -> dict:
    splits = jax.random.split(jax.random.key(seed), 6)
    tokens = centred(splits[0], (TOKENS, D), 1.0, 6.0, ((0, 32), (1, 16)))
    inner_weight = centred(splits[1], (D, FF), D ** -0.5, 0.0546875, ((0, 16), (1, 32)))
    inner_bias = centred(splits[2], (FF,), 0.5, 3.0, ((0, 32),))
    outer_weight = centred(splits[3], (FF, D), FF ** -0.5, 0.0390625, ((0, 32), (1, 16)))
    outer_bias = centred(splits[4], (D,), 0.5, 3.0, ((0, 16),))
    return {"tokens": tokens, "inner_weight": inner_weight, "inner_bias": inner_bias, "outer_weight": outer_weight, "outer_bias": outer_bias}


def rounded(product):
    return lax.optimization_barrier(product.astype(jnp.bfloat16)).astype(jnp.float32)


def blocked_product(left_matrix, right_matrix, block_count):
    block_width = left_matrix.shape[1] // block_count

    def accumulate(block_index, summed):
        begin_row = (block_index * block_width).astype(jnp.int32)
        left_piece = lax.dynamic_slice_in_dim(left_matrix, begin_row, block_width, 1)
        right_piece = lax.dynamic_slice_in_dim(right_matrix, begin_row, block_width, 0)
        return summed + rounded(jnp.dot(left_piece, right_piece, preferred_element_type=jnp.float32))

    zeros_sum = jnp.zeros((left_matrix.shape[0], right_matrix.shape[1]), jnp.float32)
    return lax.fori_loop(0, block_count, accumulate, zeros_sum)


def reference(tokens, inner_weight, inner_bias, outer_weight, outer_bias):
    preact = blocked_product(tokens, inner_weight, N_ROW) + inner_bias.astype(jnp.float32)
    hidden = jax.nn.gelu(preact, approximate=True).astype(jnp.bfloat16)
    summed = blocked_product(hidden, outer_weight, N_COL) + outer_bias.astype(jnp.float32)
    return summed.astype(jnp.bfloat16)
```

```python
import jax
import jax.numpy as jnp
from jax import lax
from jax.sharding import Mesh
from jax.sharding import PartitionSpec as P

ROW = ("zq", "zb", "c")
COL = ("y", "x", "zh")
SIZES = (4, 2, 2, 4, 4, 2)

F32 = jnp.float32
BF16 = jnp.bfloat16


def gather_by_exchange(block, axes, n):
    return lax.all_to_all(jnp.broadcast_to(block[None], (n, *block.shape)), axes, 0, 0, tiled=True)


def scatter_by_exchange(parts, axes):
    return lax.all_to_all(parts, axes, 0, 0, tiled=True).astype(F32).sum(axis=0)


def shards(tokens, w1, b1, w2, b2):
    zb, zh = lax.axis_index("zb"), lax.axis_index("zh")
    pairs = [(a, b) for a in range(2) for b in range(2)]
    straight = [(a * 2 + b, b * 2 + a) for a, b in pairs]
    crossed = [(a * 2 + b, b * 2 + 1 - a) for a, b in pairs]
    swap = [(0, 1), (1, 0)]

    got_zh = lax.ppermute(tokens, ("zb", "zh"), straight)
    got_other = lax.ppermute(tokens, ("zb", "zh"), crossed)
    mine = jnp.where(zb == zh, got_zh, got_other)
    other = jnp.where(zb == zh, got_other, got_zh)
    tok = jnp.concatenate([mine, other], axis=1)

    w1_in, tok = lax.optimization_barrier((w1, tok))
    w1_other = lax.ppermute(w1_in, "zb", swap)
    all_tok = gather_by_exchange(tok, ("y", "x"), 16).reshape(640, 1536)
    w2_in, w1_other, all_tok = lax.optimization_barrier((w2, w1_other, all_tok))
    w2_other = lax.ppermute(w2_in, "zb", swap)

    w1_pair = jnp.concatenate([w1, w1_other], axis=0)
    part = jnp.dot(all_tok, w1_pair, preferred_element_type=F32).astype(BF16)
    half = scatter_by_exchange(part.reshape(2, 320, 768), "c").astype(BF16)
    preact = scatter_by_exchange(half.reshape(4, 80, 768), "zq") + b1.astype(F32)
    hidden = jax.nn.gelu(preact, approximate=True).astype(BF16)

    hidden = gather_by_exchange(hidden, "zq", 4).reshape(320, 768)
    hidden = gather_by_exchange(hidden, "c", 2).reshape(640, 768)
    w2_pair = jnp.concatenate([w2, w2_other], axis=1)
    out = jnp.dot(hidden, w2_pair, preferred_element_type=F32).astype(BF16)
    out = scatter_by_exchange(out.reshape(16, 40, 1536), ("y", "x")).astype(BF16)

    mine, other = out[:, :768], out[:, 768:]
    back = [(b * 2 + a, (1 - a) * 2 + b) for a, b in pairs]
    to_zh = lax.ppermute(jnp.where(zb == zh, mine, other), ("zb", "zh"), straight)
    to_other = lax.ppermute(jnp.where(zb == zh, other, mine), ("zb", "zh"), back)
    return (to_zh.astype(F32) + to_other.astype(F32) + b2.astype(F32)).astype(BF16)


def solution(mesh):
    fine = Mesh(mesh.devices.reshape(SIZES), ROW + COL)
    in_specs = (P(COL, ROW), P(ROW, COL), P(COL), P(COL, ROW), P(ROW))
    return jax.shard_map(shards, mesh=fine, in_specs=in_specs, out_specs=P(COL, ROW), check_vma=False)
```

```python
import jax
import jax.numpy as jnp
from jax import lax
from jax.experimental import pallas as pl
from jax.experimental.pallas import tpu as pltpu
from jax.sharding import Mesh
from jax.sharding import PartitionSpec as P

ROW = ("zq", "zb", "c")
COL = ("yp", "y0", "xp", "x0", "zh")
SIZES = (4, 2, 2, 2, 2, 2, 2, 2)
PLANE = ("yp", "y0", "xp", "x0")
CORNER = ("zb", "c", "y0", "x0", "zh")
SWAP = [(0, 1), (1, 0)]
VMEM = pl.BlockSpec(memory_space=pltpu.VMEM)

F32 = jnp.float32
BF16 = jnp.bfloat16
barrier = lax.optimization_barrier


def corner_pairs(other_zh):
    return [(i, ((i >> 1) & 3) << 3 | (i >> 3) << 1 | ((i & 1) ^ other_zh)) for i in range(32)]


def slot(block, dz, dc):
    y0 = jnp.bitwise_xor(lax.axis_index("zb"), dz)
    x0 = jnp.bitwise_xor(lax.axis_index("c"), dc)
    return (block & 2) * 4 + y0 * 4 + (block & 1) * 2 + x0


def cost(flops, nbytes):
    return pl.CostEstimate(flops=flops, bytes_accessed=nbytes, transcendentals=0)


def first_kernel(got, w00, w01, w10, w11, p0, p1, p2, p3, total):
    for k, w in enumerate((w00, w01, w10, w11)):
        left = jnp.concatenate([got[slot(b, k // 2, k % 2)] for b in range(4)], axis=0)
        part = jnp.dot(left, w[...], preferred_element_type=F32).reshape(4, 40, 768)
        total[...] = part if k == 0 else total[...] + part
    zq = lax.axis_index("zq")
    for k, p in enumerate((p0, p1, p2, p3)):
        p[...] = total[jnp.bitwise_xor(zq, k)].astype(BF16)


def first(got, ws):
    return pl.pallas_call(
        first_kernel,
        out_shape=[jax.ShapeDtypeStruct((40, 768), BF16)] * 4,
        in_specs=[VMEM] * 5,
        out_specs=[VMEM] * 4,
        scratch_shapes=[pltpu.VMEM((4, 40, 768), F32)],
        compiler_params=pltpu.CompilerParams(vmem_limit_bytes=8 << 20),
        cost_estimate=cost(2 * 160 * 3072 * 768, 6 << 20),
        name="first_product",
    )(got, *ws)


def second_kernel(h0, h1, h2, h3, w00, w01, w10, w11, out):
    zq = lax.axis_index("zq")
    left = jnp.concatenate([h[...] for h in (h0, h1, h2, h3)], axis=0)
    for k, w in enumerate((w00, w01, w10, w11)):
        part = jnp.dot(left, w[...], preferred_element_type=F32)
        for j in range(4):
            at = slot(jnp.bitwise_xor(zq, j), k // 2, k % 2)
            out[at] = part[j * 40 : (j + 1) * 40].astype(BF16)


def second(hs, ws):
    return pl.pallas_call(
        second_kernel,
        out_shape=jax.ShapeDtypeStruct((16, 40, 768), BF16),
        in_specs=[VMEM] * 8,
        out_specs=VMEM,
        compiler_params=pltpu.CompilerParams(vmem_limit_bytes=8 << 20),
        cost_estimate=cost(2 * 160 * 3072 * 768, 6 << 20),
        name="second_product",
    )(*hs, *ws)


def across(block, k):
    return lax.ppermute(block, "zq", [(i, i ^ k) for i in range(4)])


def middle_kernel(p0, p1, p2, p3, bias, h):
    preact = bias[...].astype(F32)
    for p in (p0, p1, p2, p3):
        preact = preact + p[...].astype(F32)
    h[...] = jax.nn.gelu(preact, approximate=True).astype(BF16)


def middle(ps, bias):
    return pl.pallas_call(
        middle_kernel,
        out_shape=jax.ShapeDtypeStruct((40, 768), BF16),
        in_specs=[VMEM] * 5,
        out_specs=VMEM,
        compiler_params=pltpu.CompilerParams(vmem_limit_bytes=4 << 20),
        cost_estimate=cost(20 * 40 * 768, 5 * 40 * 768 * 2),
        name="sum_gelu",
    )(*ps, bias)


def across(block, k):
    return lax.ppermute(block, "zq", [(i, i ^ k) for i in range(4)])


def shards(tokens, w1, b1, w2, b2):
    tok = [lax.ppermute(tokens, CORNER, corner_pairs(1 - k)) for k in range(2)]

    got = []
    for k in range(2):
        if k:
            tok[k], got[0] = barrier((tok[k], got[0]))
        spread = jnp.broadcast_to(tok[k][None], (16, 40, 768))
        got.append(lax.all_to_all(spread, PLANE, 0, 0, tiled=True))

    w1_z, got[0] = barrier((lax.ppermute(w1, "zb", SWAP), got[0]))
    w1_all = [w1, lax.ppermute(w1, "c", SWAP), w1_z, lax.ppermute(w1_z, "c", SWAP)]
    w2_own, w1_z = barrier((w2, w1_z))
    w2_z = lax.ppermute(w2_own, "zb", SWAP)

    bias = b1.reshape(1, 768)
    parts = [first(g, w1_all) for g in got]
    sums = [[p[0]] + [across(p[i], i) for i in range(1, 4)] for p in parts]
    sums[0], parts[1] = barrier((sums[0], parts[1]))
    sums[1], w2_z = barrier((sums[1], w2_z))
    w2_all = [w2, lax.ppermute(w2, "c", SWAP), w2_z, lax.ppermute(w2_z, "c", SWAP)]
    hidden = [middle(s, bias) for s in sums]
    rows = [[h] + [across(h, i) for i in range(1, 4)] for h in hidden]
    rows[0], hidden[1] = barrier((rows[0], hidden[1]))
    outs = [second(r, w2_all) for r in rows]
    back = []
    for k in range(2):
        if k:
            outs[k], out = barrier((outs[k], out))
        out = lax.all_to_all(outs[k], PLANE, 0, 0, tiled=True)
        total = out.astype(F32).sum(axis=0).astype(BF16)
        back.append(lax.ppermute(total, CORNER, corner_pairs(1 - k)))
    return (back[0].astype(F32) + back[1].astype(F32) + b2.astype(F32)).astype(BF16)


def solution(mesh):
    fine = Mesh(mesh.devices.reshape(SIZES), ROW + COL)
    in_specs = (P(COL, ROW), P(ROW, COL), P(COL), P(COL, ROW), P(ROW))
    return jax.shard_map(shards, mesh=fine, in_specs=in_specs, out_specs=P(COL, ROW), check_vma=False)
```

```python
import jax
import jax.numpy as jnp
from jax import lax
from jax.experimental import pallas as pl
from jax.experimental.pallas import tpu as pltpu
from jax.sharding import Mesh
from jax.sharding import PartitionSpec as P

ROW = ("zq", "zb", "c")
COL = ("yp", "y0", "xp", "x0", "zh")
SIZES = (4, 2, 2, 2, 2, 2, 2, 2)
PLANE = ("yp", "y0", "xp", "x0")
CORNER = ("zb", "c", "y0", "x0", "zh")
SWAP = [(0, 1), (1, 0)]
VMEM = pl.BlockSpec(memory_space=pltpu.VMEM)

F32 = jnp.float32
BF16 = jnp.bfloat16
barrier = lax.optimization_barrier


def corner_pairs(other_zh):
    return [(i, ((i >> 1) & 3) << 3 | (i >> 3) << 1 | ((i & 1) ^ other_zh)) for i in range(32)]


def slot(block, dz, dc):
    y0 = jnp.bitwise_xor(lax.axis_index("zb"), dz)
    x0 = jnp.bitwise_xor(lax.axis_index("c"), dc)
    return (block & 2) * 4 + y0 * 4 + (block & 1) * 2 + x0


def kernel_call(kernel, shape, n_in, flops, nbytes, scratch=()):
    return pl.pallas_call(
        kernel,
        out_shape=jax.ShapeDtypeStruct(shape, BF16),
        in_specs=[VMEM] * n_in,
        out_specs=VMEM,
        scratch_shapes=scratch,
        compiler_params=pltpu.CompilerParams(vmem_limit_bytes=12 << 20),
        cost_estimate=pl.CostEstimate(flops=flops, bytes_accessed=nbytes, transcendentals=0),
    )


def first_kernel(got, w00, w01, w10, w11, part, total):
    for k, w in enumerate((w00, w01, w10, w11)):
        left = jnp.concatenate([got[slot(b, k // 2, k % 2)] for b in range(4)], axis=0)
        product = jnp.dot(left, w[...], preferred_element_type=F32)
        total[...] = product if k == 0 else total[...] + product
    part[...] = total[...].astype(BF16).reshape(4, 80, 768)


def middle_kernel(parts, bias, h):
    preact = bias[...].astype(F32)
    for k in range(4):
        preact = preact + parts[k].astype(F32)
    h[...] = jax.nn.gelu(preact, approximate=True).astype(BF16)


def second_kernel(hidden, w00, w01, w10, w11, out):
    left = hidden[...].reshape(320, 768)
    for k, w in enumerate((w00, w01, w10, w11)):
        product = jnp.dot(left, w[...], preferred_element_type=F32).astype(BF16)
        for b in range(4):
            out[slot(b, k // 2, k % 2)] = product[b * 80 : (b + 1) * 80]


def shards(tokens, w1, b1, w2, b2):
    tok = jnp.concatenate([lax.ppermute(tokens, CORNER, corner_pairs(k)) for k in range(2)], axis=0)
    w1_in, w2_in, tok = barrier((w1, w2, tok))

    def weights(w):
        w_z = lax.ppermute(w, "zb", SWAP)
        return [w, lax.ppermute(w, "c", SWAP), w_z, lax.ppermute(w_z, "c", SWAP)]

    w1_all = weights(w1_in)
    w2_all = weights(w2_in)

    spread = jnp.broadcast_to(tok[None], (16, 80, 768))
    got = lax.all_to_all(spread, PLANE, 0, 0, tiled=True)
    flops = 2 * 320 * 3072 * 768
    scratch = [pltpu.VMEM((320, 768), F32)]
    part = kernel_call(first_kernel, (4, 80, 768), 5, flops, 8 << 20, scratch)(got, *w1_all)
    part = lax.all_to_all(part, "zq", 0, 0, tiled=True)
    h = kernel_call(middle_kernel, (80, 768), 2, 20 * 80 * 768, 1 << 20)(part, b1.reshape(1, 768))
    hidden = lax.all_gather(h, "zq", axis=0, tiled=False)
    out = kernel_call(second_kernel, (16, 80, 768), 5, flops, 8 << 20)(hidden, *w2_all)
    out = lax.all_to_all(out, PLANE, 0, 0, tiled=True).astype(F32).sum(axis=0).astype(BF16)

    back = [lax.ppermute(out[k * 40 : (k + 1) * 40], CORNER, corner_pairs(k)) for k in range(2)]
    return (back[0].astype(F32) + back[1].astype(F32) + b2.astype(F32)).astype(BF16)


def solution(mesh):
    fine = Mesh(mesh.devices.reshape(SIZES), ROW + COL)
    in_specs = (P(COL, ROW), P(ROW, COL), P(COL), P(COL, ROW), P(ROW))
    return jax.shard_map(shards, mesh=fine, in_specs=in_specs, out_specs=P(COL, ROW), check_vma=False)
```

```python
import jax
import jax.numpy as jnp
from jax import lax
from jax.experimental import pallas as pl
from jax.experimental.pallas import tpu as pltpu
from jax.sharding import Mesh
from jax.sharding import PartitionSpec as P

ROW = ("zq", "zb", "c")
COL = ("yp", "y0", "xp", "x0", "zh")
SIZES = (4, 2, 2, 2, 2, 2, 2, 2)
PLANE = ("yp", "y0", "xp", "x0")
CORNER = ("zb", "c", "y0", "x0", "zh")
SWAP = [(0, 1), (1, 0)]
EARLY = 256
VMEM = pl.BlockSpec(memory_space=pltpu.VMEM)
ANY = pl.BlockSpec(memory_space=pl.ANY)

F32 = jnp.float32
BF16 = jnp.bfloat16
barrier = lax.optimization_barrier


def corner_pairs(other_zh):
    return [(i, ((i >> 1) & 3) << 3 | (i >> 3) << 1 | ((i & 1) ^ other_zh)) for i in range(32)]


def slot(block, dz, dc):
    y0 = jnp.bitwise_xor(lax.axis_index("zb"), dz)
    x0 = jnp.bitwise_xor(lax.axis_index("c"), dc)
    return (block & 2) * 4 + y0 * 4 + (block & 1) * 2 + x0


def kernel_call(kernel, shapes, specs, flops, nbytes, scratch=(), limit=16):
    return pl.pallas_call(
        kernel,
        out_shape=shapes,
        in_specs=specs,
        out_specs=[VMEM] * len(shapes),
        scratch_shapes=scratch,
        compiler_params=pltpu.CompilerParams(vmem_limit_bytes=limit << 20),
        cost_estimate=pl.CostEstimate(flops=flops, bytes_accessed=nbytes, transcendentals=0),
    )


def fetch(pairs, sems):
    copies = [pltpu.make_async_copy(src, dst, sems.at[i]) for i, (src, dst) in enumerate(pairs)]
    for copy in copies:
        copy.start()
    return copies


def parts_of(blocks, held):
    if not isinstance(blocks, tuple):
        return [(blocks, held)]
    return [(blocks[0], held.at[:EARLY]), (blocks[1], held.at[EARLY:])]


def held_blocks(n):
    return [pltpu.VMEM((n, 768, 768), BF16), pltpu.SemaphoreType.DMA((n, 2))]


def left_blocks(n):
    return [pltpu.VMEM((n, 320, 768), BF16), pltpu.SemaphoreType.DMA((n, 4))]


def products(got, ks, blocks, left, left_sems, held, sems):
    copies = []
    for i, k in enumerate(ks):
        rows = [(got.at[slot(b, k // 2, k % 2)], left.at[i, b * 80 : (b + 1) * 80]) for b in range(4)]
        copies.append(fetch(rows, left_sems.at[i]) + fetch(parts_of(blocks[i], held.at[i]), sems.at[i]))
    for i in range(len(ks)):
        for copy in copies[i]:
            copy.wait()
        yield jnp.dot(left[i], held[i], preferred_element_type=F32)


def first_kernel(got, w00, w01, w10a, w10b, total, *scratch):
    for k, product in enumerate(products(got, (0, 1, 2), (w00, w01, (w10a, w10b)), *scratch)):
        total[...] = product if k == 0 else total[...] + product


def first_rest_kernel(got, w11a, w11b, total, part, *scratch):
    (product,) = products(got, (3,), ((w11a, w11b),), *scratch)
    part[...] = (total[...] + product).astype(BF16).reshape(4, 80, 768)


def middle_kernel(parts, bias, here, other):
    preact = bias[...].astype(F32)
    for k in range(4):
        preact = preact + parts[k].astype(F32)
    h = jax.nn.gelu(preact, approximate=True).astype(BF16)
    here[...] = h[:40]
    other[...] = h[40:]


def spread_product(left, first_block, blocks, out, held, sems):
    copies = [fetch(parts_of(block, held.at[k]), sems.at[k]) for k, block in enumerate(blocks)]
    for k in range(4):
        for copy in copies[k]:
            copy.wait()
        product = jnp.dot(left, held[k], preferred_element_type=F32)
        for j in range(4):
            rows = product[j * 40 : (j + 1) * 40]
            out[slot(jnp.bitwise_xor(first_block, j), k // 2, k % 2)] = rows.astype(BF16)


def second_kernel(h0, h1, h2, h3, w00, w01, w10, w11, out, held, sems):
    left = jnp.concatenate([h[...] for h in (h0, h1, h2, h3)], axis=0)
    spread_product(left, lax.axis_index("zq"), (w00, w01, w10, w11), out, held, sems)


def second_gathered_kernel(hidden, w00, w01, w10, w11, out, held, sems):
    left = jnp.concatenate([hidden[j] for j in range(4)], axis=0)
    spread_product(left, 0, (w00, w01, w10, w11), out, held, sems)


def shards(tokens, w1, b1, w2, b2):
    here, other = (lax.ppermute(tokens, CORNER, corner_pairs(k)) for k in range(2))
    w1_za = lax.ppermute(w1[:EARLY], "zb", SWAP)
    here, other, w1_za = barrier((here, other, w1_za))
    w1_in, here = barrier((w1, here))
    w1_zb = lax.ppermute(w1_in[EARLY:], "zb", SWAP)
    w1_c = lax.ppermute(w1_in, "c", SWAP)
    w1_zca = lax.ppermute(w1_za, "c", SWAP)

    tok = jnp.concatenate([here, other], axis=0)
    spread = jnp.broadcast_to(tok[None], (16, 80, 768))
    got = lax.all_to_all(spread, PLANE, 0, 0, tiled=True)
    w2_in, w1_zca = barrier((w2, w1_zca))
    w1_zb, w1_zca, w1_c, got = barrier((w1_zb, w1_zca, w1_c, got))
    w1_zcb = lax.ppermute(w1_zb, "c", SWAP)
    w2_z = lax.ppermute(w2_in, "zb", SWAP)

    flops = 2 * 320 * 768 * 768
    shapes = [jax.ShapeDtypeStruct((320, 768), F32)]
    scratch = left_blocks(3) + held_blocks(3)
    first = kernel_call(first_kernel, shapes, [ANY] * 5, 3 * flops, 8 << 20, scratch, 60)
    (total,) = first(got, w1, w1_c, w1_za, w1_zb)
    shapes = [jax.ShapeDtypeStruct((4, 80, 768), BF16)]
    scratch = left_blocks(1) + held_blocks(1)
    first_rest = kernel_call(first_rest_kernel, shapes, [ANY] * 3 + [VMEM], flops, 3 << 20, scratch, 60)
    (part,) = first_rest(got, w1_zca, w1_zcb, total)
    w2_all = [w2, lax.ppermute(w2_in, "c", SWAP), w2_z, lax.ppermute(w2_z, "c", SWAP)]

    part = lax.all_to_all(part, "zq", 0, 0, tiled=True)
    shapes = [jax.ShapeDtypeStruct((40, 768), BF16)] * 2
    here, other = kernel_call(middle_kernel, shapes, [VMEM] * 2, 20 * 80 * 768, 1 << 20)(part, b1.reshape(1, 768))

    flops = 2 * 160 * 3072 * 768
    shapes = [jax.ShapeDtypeStruct((16, 40, 768), BF16)]
    hidden = lax.all_gather(other, "zq", axis=0, tiled=False)
    here, hidden = barrier((here, hidden))
    rows = [here] + [lax.ppermute(here, "zq", [(i, i ^ k) for i in range(4)]) for k in range(1, 4)]
    specs = [VMEM] + [ANY] * 4
    (out,) = kernel_call(second_gathered_kernel, shapes, specs, flops, 6 << 20, held_blocks(4))(hidden, *w2_all)
    other = lax.all_to_all(out, PLANE, 0, 0, tiled=True)
    specs = [VMEM] * 4 + [ANY] * 4
    (out,) = kernel_call(second_kernel, shapes, specs, flops, 6 << 20, held_blocks(4))(*rows, *w2_all)
    out, other = barrier((out, other))
    here = lax.all_to_all(out, PLANE, 0, 0, tiled=True)

    total = b2.astype(F32)
    for k, out in ((1, other), (0, here)):
        out = out.astype(F32).sum(axis=0).astype(BF16)
        total = total + lax.ppermute(out, CORNER, corner_pairs(k)).astype(F32)
    return total.astype(BF16)


def solution(mesh):
    fine = Mesh(mesh.devices.reshape(SIZES), ROW + COL)
    in_specs = (P(COL, ROW), P(ROW, COL), P(COL), P(COL, ROW), P(ROW))
    return jax.shard_map(shards, mesh=fine, in_specs=in_specs, out_specs=P(COL, ROW), check_vma=False)
```

```python
import jax
import jax.numpy as jnp
from jax import lax
from jax.experimental import pallas as pl
from jax.experimental.pallas import tpu as pltpu
from jax.sharding import Mesh
from jax.sharding import PartitionSpec as P

ROW = ("zq", "zb", "c")
COL = ("yp", "y0", "xp", "x0", "zh")
SIZES = (4, 2, 2, 2, 2, 2, 2, 2)
PLANE = ("yp", "y0", "xp", "x0")
CORNER = ("zb", "c", "y0", "x0", "zh")
SWAP = [(0, 1), (1, 0)]
VMEM = pl.BlockSpec(memory_space=pltpu.VMEM)
ANY = pl.BlockSpec(memory_space=pl.ANY)

F32 = jnp.float32
BF16 = jnp.bfloat16
barrier = lax.optimization_barrier


def corner_pairs(other_zh):
    return [(i, ((i >> 1) & 3) << 3 | (i >> 3) << 1 | ((i & 1) ^ other_zh)) for i in range(32)]


def slot(block, dz, dc):
    y0 = jnp.bitwise_xor(lax.axis_index("zb"), dz)
    x0 = jnp.bitwise_xor(lax.axis_index("c"), dc)
    return (block & 2) * 4 + y0 * 4 + (block & 1) * 2 + x0


def kernel_call(kernel, shape, specs, out_spec, cost, scratch=(), limit=16):
    flops, nbytes = cost
    return pl.pallas_call(
        kernel,
        out_shape=jax.ShapeDtypeStruct(shape, BF16),
        in_specs=specs,
        out_specs=out_spec,
        scratch_shapes=scratch,
        compiler_params=pltpu.CompilerParams(vmem_limit_bytes=limit << 20),
        cost_estimate=pl.CostEstimate(flops=flops, bytes_accessed=nbytes, transcendentals=0),
    )


def start_all(pairs, sems):
    copies = [pltpu.make_async_copy(src, dst, sems.at[i]) for i, (src, dst) in enumerate(pairs)]
    for copy in copies:
        copy.start()
    return copies


def spread_kernel(here, other, out, block, sems):
    block[:40] = here[...]
    block[40:] = other[...]
    for copy in start_all([(block, out.at[i]) for i in range(16)], sems):
        copy.wait()


def first_kernel(got, w00, w01, w10, w11, part, total, held, sems):
    copies = start_all([(w00, held.at[0]), (w01, held.at[1])], sems)
    for i, k in enumerate((2, 3, 0, 1)):
        left = jnp.concatenate([got[slot(b, k // 2, k % 2)] for b in range(4)], axis=0)
        if k < 2:
            copies[k].wait()
        right = (w10[...], w11[...])[i] if k > 1 else held[k]
        product = jnp.dot(left, right, preferred_element_type=F32)
        if i < 3:
            total[...] = product if i == 0 else total[...] + product
        else:
            part[...] = (total[...] + product).astype(BF16).reshape(4, 80, 768)


def middle_kernel(parts, bias, h):
    preact = bias[...].astype(F32)
    for k in range(4):
        preact = preact + parts[k].astype(F32)
    h[...] = jax.nn.gelu(preact, approximate=True).astype(BF16)


def second_kernel(h0, h1, h2, h3, w00, w01, w10, w11, out, held, sems):
    copies = start_all([(w00, held.at[0]), (w01, held.at[1])], sems)
    zq = lax.axis_index("zq")
    left = jnp.concatenate([h[...] for h in (h0, h1, h2, h3)], axis=0)
    for i, k in enumerate((2, 3, 0, 1)):
        if k < 2:
            copies[k].wait()
        right = (w10[...], w11[...])[i] if k > 1 else held[k]
        product = jnp.dot(left, right, preferred_element_type=F32)
        for j in range(4):
            rows = product[j * 80 : (j + 1) * 80]
            out[slot(jnp.bitwise_xor(zq, j), k // 2, k % 2)] = rows.astype(BF16)


def shards(tokens, w1, b1, w2, b2):
    here, other = (lax.ppermute(tokens, CORNER, corner_pairs(k)) for k in range(2))
    w1_in, here = barrier((w1, here))
    w2_in, here = barrier((w2, here))

    def weights(w):
        w_z = lax.ppermute(w, "zb", SWAP)
        return [w, lax.ppermute(w, "c", SWAP), w_z, lax.ppermute(w_z, "c", SWAP)]

    w1_all = weights(w1_in)
    w2_all = weights(w2_in)

    scratch = [pltpu.VMEM((80, 768), BF16), pltpu.SemaphoreType.DMA((16,))]
    spread = kernel_call(spread_kernel, (16, 80, 768), [VMEM] * 2, ANY, (5 * 10**9, 4 << 20), scratch)(here, other)
    got = lax.all_to_all(spread, PLANE, 0, 0, tiled=True)

    held = [pltpu.VMEM((2, 768, 768), BF16), pltpu.SemaphoreType.DMA((2,))]
    weight_specs = [ANY, ANY, VMEM, VMEM]
    cost = (2 * 320 * 3072 * 768, 8 << 20)
    scratch = [pltpu.VMEM((320, 768), F32)] + held
    first = kernel_call(first_kernel, (4, 80, 768), [VMEM] + weight_specs, VMEM, cost, scratch, 54)
    part = lax.all_to_all(first(got, *w1_all), "zq", 0, 0, tiled=True)
    middle = kernel_call(middle_kernel, (80, 768), [VMEM] * 2, VMEM, (20 * 80 * 768, 1 << 20))
    h = middle(part, b1.reshape(1, 768))
    rows = [h] + [lax.ppermute(h, "zq", [(i, i ^ k) for i in range(4)]) for k in range(1, 4)]
    second = kernel_call(second_kernel, (16, 80, 768), [VMEM] * 4 + weight_specs, VMEM, cost, held, 50)
    out = lax.all_to_all(second(*rows, *w2_all), PLANE, 0, 0, tiled=True)
    out = out.astype(F32).sum(axis=0).astype(BF16)

    back = [lax.ppermute(out[k * 40 : (k + 1) * 40], CORNER, corner_pairs(k)) for k in range(2)]
    return (back[0].astype(F32) + back[1].astype(F32) + b2.astype(F32)).astype(BF16)


def solution(mesh):
    fine = Mesh(mesh.devices.reshape(SIZES), ROW + COL)
    in_specs = (P(COL, ROW), P(ROW, COL), P(COL), P(COL, ROW), P(ROW))
    return jax.shard_map(shards, mesh=fine, in_specs=in_specs, out_specs=P(COL, ROW), check_vma=False)
```

```python
import jax
import jax.numpy as jnp
from jax import lax
from jax.experimental import pallas as pl
from jax.experimental.pallas import tpu as pltpu
from jax.sharding import Mesh
from jax.sharding import PartitionSpec as P

ROW = ("zq", "zb", "c")
COL = ("yp", "y0", "xp", "x0", "zh")
SIZES = (4, 2, 2, 2, 2, 2, 2, 2)
PLANE = ("yp", "y0", "xp", "x0")
CORNER = ("zb", "c", "y0", "x0", "zh")
SWAP = [(0, 1), (1, 0)]
VMEM = pl.BlockSpec(memory_space=pltpu.VMEM)

F32 = jnp.float32
BF16 = jnp.bfloat16
barrier = lax.optimization_barrier


def corner_pairs(other_zh):
    return [(i, ((i >> 1) & 3) << 3 | (i >> 3) << 1 | ((i & 1) ^ other_zh)) for i in range(32)]


def slot(block, dz, dc):
    y0 = jnp.bitwise_xor(lax.axis_index("zb"), dz)
    x0 = jnp.bitwise_xor(lax.axis_index("c"), dc)
    return (block & 2) * 4 + y0 * 4 + (block & 1) * 2 + x0


def kernel_call(kernel, shapes, n_in, flops, nbytes, scratch=(), limit=12):
    return pl.pallas_call(
        kernel,
        out_shape=[jax.ShapeDtypeStruct(shape, BF16) for shape in shapes],
        in_specs=[VMEM] * n_in,
        out_specs=[VMEM] * len(shapes),
        scratch_shapes=scratch,
        compiler_params=pltpu.CompilerParams(vmem_limit_bytes=limit << 20),
        cost_estimate=pl.CostEstimate(flops=flops, bytes_accessed=nbytes, transcendentals=0),
    )


def first_kernel(got, w00, w01, w10, w11, part, total):
    for k, w in enumerate((w00, w01, w10, w11)):
        left = jnp.concatenate([got[slot(b, k // 2, k % 2)] for b in range(4)], axis=0)
        product = jnp.dot(left, w[...], preferred_element_type=F32)
        total[...] = product if k == 0 else total[...] + product
    part[...] = total[...].astype(BF16).reshape(4, 80, 768)


def middle_kernel(parts, bias, h):
    preact = bias[...].astype(F32)
    for k in range(4):
        preact = preact + parts[k].astype(F32)
    h[...] = jax.nn.gelu(preact, approximate=True).astype(BF16)


def second_kernel(hidden, w00, w01, w10, w11, here, other):
    for half, out in ((1, other), (0, here)):
        left = jnp.concatenate([hidden[b, half * 40 : (half + 1) * 40] for b in range(4)], axis=0)
        for k, w in enumerate((w00, w01, w10, w11)):
            product = jnp.dot(left, w[...], preferred_element_type=F32).astype(BF16)
            for b in range(4):
                out[slot(b, k // 2, k % 2)] = product[b * 40 : (b + 1) * 40]


def shards(tokens, w1, b1, w2, b2):
    tok = jnp.concatenate([lax.ppermute(tokens, CORNER, corner_pairs(k)) for k in range(2)], axis=0)
    w1_in, w2_in, tok = barrier((w1, w2, tok))

    def weights(w):
        w_z = lax.ppermute(w, "zb", SWAP)
        return [w, lax.ppermute(w, "c", SWAP), w_z, lax.ppermute(w_z, "c", SWAP)]

    w1_all = weights(w1_in)
    w2_all = weights(w2_in)

    spread = jnp.broadcast_to(tok[None], (16, 80, 768))
    got = lax.all_to_all(spread, PLANE, 0, 0, tiled=True)
    flops = 2 * 320 * 3072 * 768
    scratch = [pltpu.VMEM((320, 768), F32)]
    (part,) = kernel_call(first_kernel, [(4, 80, 768)], 5, flops, 8 << 20, scratch, 54)(got, *w1_all)
    part = lax.all_to_all(part, "zq", 0, 0, tiled=True)
    (h,) = kernel_call(middle_kernel, [(80, 768)], 2, 20 * 80 * 768, 1 << 20)(part, b1.reshape(1, 768))
    hidden = lax.all_gather(h, "zq", axis=0, tiled=False)
    shapes = [(16, 40, 768)] * 2
    here, other = kernel_call(second_kernel, shapes, 5, flops, 8 << 20, (), 12)(hidden, *w2_all)

    other = lax.all_to_all(other, PLANE, 0, 0, tiled=True)
    here, _ = barrier((here, other))
    here = lax.all_to_all(here, PLANE, 0, 0, tiled=True)
    total = b2.astype(F32)
    for k, out in ((1, other), (0, here)):
        out = out.astype(F32).sum(axis=0).astype(BF16)
        total = total + lax.ppermute(out, CORNER, corner_pairs(k)).astype(F32)
    return total.astype(BF16)


def solution(mesh):
    fine = Mesh(mesh.devices.reshape(SIZES), ROW + COL)
    in_specs = (P(COL, ROW), P(ROW, COL), P(COL), P(COL, ROW), P(ROW))
    return jax.shard_map(shards, mesh=fine, in_specs=in_specs, out_specs=P(COL, ROW), check_vma=False)
```

```python
import jax
import jax.numpy as jnp
from jax import lax
from jax.experimental import pallas as pl
from jax.experimental.pallas import tpu as pltpu
from jax.sharding import Mesh
from jax.sharding import PartitionSpec as P

ROW = ("zq", "zb", "c")
COL = ("yp", "y0", "xp", "x0", "zh")
SIZES = (4, 2, 2, 2, 2, 2, 2, 2)
PLANE = ("yp", "y0", "xp", "x0")
CORNER = ("zb", "c", "y0", "x0", "zh")
SWAP = [(0, 1), (1, 0)]
VMEM = pl.BlockSpec(memory_space=pltpu.VMEM)

F32 = jnp.float32
BF16 = jnp.bfloat16
barrier = lax.optimization_barrier


def corner_pairs(other_zh):
    return [(i, ((i >> 1) & 3) << 3 | (i >> 3) << 1 | ((i & 1) ^ other_zh)) for i in range(32)]


def slot(block, dz, dc):
    y0 = jnp.bitwise_xor(lax.axis_index("zb"), dz)
    x0 = jnp.bitwise_xor(lax.axis_index("c"), dc)
    return (block & 2) * 4 + y0 * 4 + (block & 1) * 2 + x0


def kernel_call(kernel, shapes, n_in, flops, nbytes, scratch=(), limit=12):
    return pl.pallas_call(
        kernel,
        out_shape=[jax.ShapeDtypeStruct(shape, BF16) for shape in shapes],
        in_specs=[VMEM] * n_in,
        out_specs=[VMEM] * len(shapes),
        scratch_shapes=scratch,
        compiler_params=pltpu.CompilerParams(vmem_limit_bytes=limit << 20),
        cost_estimate=pl.CostEstimate(flops=flops, bytes_accessed=nbytes, transcendentals=0),
    )


def spread_kernel(block, out):
    for i in range(16):
        out[i] = block[...]


def first_kernel(here, other, w00, w01, w10, w11a, w11b, part, total):
    for k, ws in enumerate(((w00,), (w01,), (w10,), (w11a, w11b))):
        rows = [got[slot(b, k // 2, k % 2)] for b in range(4) for got in (here, other)]
        left = jnp.concatenate(rows, axis=0)
        right = ws[0][...] if k < 3 else jnp.concatenate([w[...] for w in ws], axis=0)
        product = jnp.dot(left, right, preferred_element_type=F32)
        total[...] = product if k == 0 else total[...] + product
    part[...] = total[...].astype(BF16).reshape(4, 80, 768)


def middle_kernel(parts, bias, h):
    preact = bias[...].astype(F32)
    for k in range(4):
        preact = preact + parts[k].astype(F32)
    h[...] = jax.nn.gelu(preact, approximate=True).astype(BF16)


def second_kernel(hidden, w00, w01, w10, w11, here, other):
    for half, out in ((1, other), (0, here)):
        left = jnp.concatenate([hidden[b, half * 40 : (half + 1) * 40] for b in range(4)], axis=0)
        for k, w in enumerate((w00, w01, w10, w11)):
            product = jnp.dot(left, w[...], preferred_element_type=F32).astype(BF16)
            for b in range(4):
                out[slot(b, k // 2, k % 2)] = product[b * 40 : (b + 1) * 40]


def shards(tokens, w1, b1, w2, b2):
    here, other = (lax.ppermute(tokens, CORNER, corner_pairs(k)) for k in range(2))
    w1_in, w2_in, here = barrier((w1, w2, here))

    shape = [(16, 40, 768)]
    (here,) = kernel_call(spread_kernel, shape, 1, 10**9, 1 << 20)(here)
    (other,) = kernel_call(spread_kernel, shape, 1, 40 * 10**9, 1 << 20)(other)
    here = lax.all_to_all(here, PLANE, 0, 0, tiled=True)
    other, _ = barrier((other, here))
    other = lax.all_to_all(other, PLANE, 0, 0, tiled=True)

    w1_z = lax.ppermute(w1_in, "zb", SWAP)
    w1_all = [w1, lax.ppermute(w1_in, "c", SWAP), w1_z]
    w1_all += [lax.ppermute(w1_z[at : at + 384], "c", SWAP) for at in (0, 384)]
    w2_z = lax.ppermute(w2_in, "zb", SWAP)
    w2_all = [w2, lax.ppermute(w2_in, "c", SWAP), w2_z, lax.ppermute(w2_z, "c", SWAP)]

    flops = 2 * 320 * 3072 * 768
    scratch = [pltpu.VMEM((320, 768), F32)]
    (part,) = kernel_call(first_kernel, [(4, 80, 768)], 7, flops, 8 << 20, scratch, 54)(here, other, *w1_all)
    part = lax.all_to_all(part, "zq", 0, 0, tiled=True)
    (h,) = kernel_call(middle_kernel, [(80, 768)], 2, 20 * 80 * 768, 1 << 20)(part, b1.reshape(1, 768))
    hidden = lax.all_gather(h, "zq", axis=0, tiled=False)
    shapes = [(16, 40, 768)] * 2
    here, other = kernel_call(second_kernel, shapes, 5, flops, 8 << 20, (), 12)(hidden, *w2_all)

    other = lax.all_to_all(other, PLANE, 0, 0, tiled=True)
    here, _ = barrier((here, other))
    here = lax.all_to_all(here, PLANE, 0, 0, tiled=True)
    total = b2.astype(F32)
    for k, out in ((1, other), (0, here)):
        out = out.astype(F32).sum(axis=0).astype(BF16)
        total = total + lax.ppermute(out, CORNER, corner_pairs(k)).astype(F32)
    return total.astype(BF16)


def solution(mesh):
    fine = Mesh(mesh.devices.reshape(SIZES), ROW + COL)
    in_specs = (P(COL, ROW), P(ROW, COL), P(COL), P(COL, ROW), P(ROW))
    return jax.shard_map(shards, mesh=fine, in_specs=in_specs, out_specs=P(COL, ROW), check_vma=False)
```

```python
import jax
import jax.numpy as jnp
from jax import lax
from jax.experimental import pallas as pl
from jax.experimental.pallas import tpu as pltpu
from jax.sharding import Mesh
from jax.sharding import PartitionSpec as P

ROW = ("zq", "zb", "c")
COL = ("yp", "y0", "xp", "x0", "zh")
SIZES = (4, 2, 2, 2, 2, 2, 2, 2)
PLANE = ("yp", "y0", "xp", "x0")
CORNER = ("zb", "c", "y0", "x0", "zh")
SWAP = [(0, 1), (1, 0)]
VMEM = pl.BlockSpec(memory_space=pltpu.VMEM)

F32 = jnp.float32
BF16 = jnp.bfloat16
barrier = lax.optimization_barrier


def corner_pairs(other_zh):
    return [(i, ((i >> 1) & 3) << 3 | (i >> 3) << 1 | ((i & 1) ^ other_zh)) for i in range(32)]


def slot(block, dz, dc):
    y0 = jnp.bitwise_xor(lax.axis_index("zb"), dz)
    x0 = jnp.bitwise_xor(lax.axis_index("c"), dc)
    return (block & 2) * 4 + y0 * 4 + (block & 1) * 2 + x0


def kernel_call(kernel, shapes, n_in, flops, nbytes, scratch=(), limit=12):
    return pl.pallas_call(
        kernel,
        out_shape=[jax.ShapeDtypeStruct(shape, BF16) for shape in shapes],
        in_specs=[VMEM] * n_in,
        out_specs=[VMEM] * len(shapes),
        scratch_shapes=scratch,
        compiler_params=pltpu.CompilerParams(vmem_limit_bytes=limit << 20),
        cost_estimate=pl.CostEstimate(flops=flops, bytes_accessed=nbytes, transcendentals=0),
    )


def spread_kernel(block, out):
    for i in range(16):
        out[i] = block[...]


def first_kernel(here, other, w00, w01, w10, w11a, w11b, part, total):
    for k, ws in enumerate(((w00,), (w01,), (w10,), (w11a, w11b))):
        rows = [got[slot(b, k // 2, k % 2)] for b in range(4) for got in (here, other)]
        left = jnp.concatenate(rows, axis=0)
        right = ws[0][...] if k < 3 else jnp.concatenate([w[...] for w in ws], axis=0)
        product = jnp.dot(left, right, preferred_element_type=F32)
        total[...] = product if k == 0 else total[...] + product
    part[...] = total[...].astype(BF16).reshape(4, 80, 768)


def middle_kernel(parts, bias, h):
    preact = bias[...].astype(F32)
    for k in range(4):
        preact = preact + parts[k].astype(F32)
    h[...] = jax.nn.gelu(preact, approximate=True).astype(BF16)


def second_kernel(hidden, w00, w01, w10, w11, here, other):
    for half, out in ((1, other), (0, here)):
        left = jnp.concatenate([hidden[b, half * 40 : (half + 1) * 40] for b in range(4)], axis=0)
        for k, w in enumerate((w00, w01, w10, w11)):
            product = jnp.dot(left, w[...], preferred_element_type=F32).astype(BF16)
            for b in range(4):
                out[slot(b, k // 2, k % 2)] = product[b * 40 : (b + 1) * 40]


def shards(tokens, w1, b1, w2, b2):
    here, other = (lax.ppermute(tokens, CORNER, corner_pairs(k)) for k in range(2))
    w1_in, w2_in, here = barrier((w1, w2, here))

    shape = [(16, 40, 768)]
    (here,) = kernel_call(spread_kernel, shape, 1, 10**9, 1 << 20)(here)
    (other,) = kernel_call(spread_kernel, shape, 1, 40 * 10**9, 1 << 20)(other)
    here = lax.all_to_all(here, PLANE, 0, 0, tiled=True)
    other, _ = barrier((other, here))
    other = lax.all_to_all(other, PLANE, 0, 0, tiled=True)

    w1_z = lax.ppermute(w1_in, "zb", SWAP)
    w1_all = [w1, lax.ppermute(w1_in, "c", SWAP), w1_z]
    w1_all += [lax.ppermute(w1_z[at : at + 384], "c", SWAP) for at in (0, 384)]
    w2_z = lax.ppermute(w2_in, "zb", SWAP)
    w2_all = [w2, lax.ppermute(w2_in, "c", SWAP), w2_z, lax.ppermute(w2_z, "c", SWAP)]

    flops = 2 * 320 * 3072 * 768
    scratch = [pltpu.VMEM((320, 768), F32)]
    (part,) = kernel_call(first_kernel, [(4, 80, 768)], 7, flops, 8 << 20, scratch, 54)(here, other, *w1_all)
    part, _ = barrier((part, w2_z))
    part = lax.all_to_all(part, "zq", 0, 0, tiled=True)
    (h,) = kernel_call(middle_kernel, [(80, 768)], 2, 20 * 80 * 768, 1 << 20)(part, b1.reshape(1, 768))
    hidden = lax.all_gather(h, "zq", axis=0, tiled=False)
    shapes = [(16, 40, 768)] * 2
    here, other = kernel_call(second_kernel, shapes, 5, flops, 8 << 20, (), 12)(hidden, *w2_all)

    other = lax.all_to_all(other, PLANE, 0, 0, tiled=True)
    here, _ = barrier((here, other))
    here = lax.all_to_all(here, PLANE, 0, 0, tiled=True)
    total = b2.astype(F32)
    for k, out in ((1, other), (0, here)):
        out = out.astype(F32).sum(axis=0).astype(BF16)
        total = total + lax.ppermute(out, CORNER, corner_pairs(k)).astype(F32)
    return total.astype(BF16)


def solution(mesh):
    fine = Mesh(mesh.devices.reshape(SIZES), ROW + COL)
    in_specs = (P(COL, ROW), P(ROW, COL), P(COL), P(COL, ROW), P(ROW))
    return jax.shard_map(shards, mesh=fine, in_specs=in_specs, out_specs=P(COL, ROW), check_vma=False)
```

```python
import jax
import jax.numpy as jnp
from jax import lax
from jax.experimental import pallas as pl
from jax.experimental.pallas import tpu as pltpu
from jax.sharding import Mesh
from jax.sharding import PartitionSpec as P

ROW = ("zq", "zb", "c")
COL = ("yp", "y0", "xp", "x0", "zh")
SIZES = (4, 2, 2, 2, 2, 2, 2, 2)
PLANE = ("yp", "y0", "xp", "x0")
CORNER = ("zb", "c", "y0", "x0", "zh")
SWAP = [(0, 1), (1, 0)]
VMEM = pl.BlockSpec(memory_space=pltpu.VMEM)

F32 = jnp.float32
BF16 = jnp.bfloat16
barrier = lax.optimization_barrier


def corner_pairs(other_zh):
    return [(i, ((i >> 1) & 3) << 3 | (i >> 3) << 1 | ((i & 1) ^ other_zh)) for i in range(32)]


def slot(block, dz, dc):
    y0 = jnp.bitwise_xor(lax.axis_index("zb"), dz)
    x0 = jnp.bitwise_xor(lax.axis_index("c"), dc)
    return (block & 2) * 4 + y0 * 4 + (block & 1) * 2 + x0


def kernel_call(kernel, shapes, n_in, flops, nbytes, scratch=(), limit=12):
    return pl.pallas_call(
        kernel,
        out_shape=[jax.ShapeDtypeStruct(shape, BF16) for shape in shapes],
        in_specs=[VMEM] * n_in,
        out_specs=[VMEM] * len(shapes),
        scratch_shapes=scratch,
        compiler_params=pltpu.CompilerParams(vmem_limit_bytes=limit << 20),
        cost_estimate=pl.CostEstimate(flops=flops, bytes_accessed=nbytes, transcendentals=0),
    )


def spread_kernel(block, out):
    for i in range(16):
        out[i] = block[...]


def first_kernel(here, other, w00, w01, w10, w11a, w11b, part, total):
    for k, ws in enumerate(((w00,), (w01,), (w10,), (w11a, w11b))):
        rows = [got[slot(b, k // 2, k % 2)] for b in range(4) for got in (here, other)]
        left = jnp.concatenate(rows, axis=0)
        right = ws[0][...] if k < 3 else jnp.concatenate([w[...] for w in ws], axis=0)
        product = jnp.dot(left, right, preferred_element_type=F32)
        total[...] = product if k == 0 else total[...] + product
    part[...] = total[...].astype(BF16).reshape(4, 80, 768)


def middle_kernel(parts, bias, h):
    preact = bias[...].astype(F32)
    for k in range(4):
        preact = preact + parts[k].astype(F32)
    h[...] = jax.nn.gelu(preact, approximate=True).astype(BF16)


def second_kernel(hidden, w00, w01, w10, w11, here, other):
    for half, out in ((1, other), (0, here)):
        left = jnp.concatenate([hidden[b, half * 40 : (half + 1) * 40] for b in range(4)], axis=0)
        for k, w in enumerate((w00, w01, w10, w11)):
            product = jnp.dot(left, w[...], preferred_element_type=F32).astype(BF16)
            for b in range(4):
                out[slot(b, k // 2, k % 2)] = product[b * 40 : (b + 1) * 40]


def shards(tokens, w1, b1, w2, b2):
    here, other = (lax.ppermute(tokens, CORNER, corner_pairs(k)) for k in range(2))
    w1_in, w2_in, here = barrier((w1, w2, here))

    shape = [(16, 40, 768)]
    (here,) = kernel_call(spread_kernel, shape, 1, 10**9, 1 << 20)(here)
    (other,) = kernel_call(spread_kernel, shape, 1, 40 * 10**9, 1 << 20)(other)
    here = lax.all_to_all(here, PLANE, 0, 0, tiled=True)
    w1_late, _ = barrier((w1, other))
    other, _ = barrier((other, here))
    other = lax.all_to_all(other, PLANE, 0, 0, tiled=True)

    w1_z = lax.ppermute(w1_in, "zb", SWAP)
    w1_all = [w1, lax.ppermute(w1_late, "c", SWAP), w1_z]
    w1_all += [lax.ppermute(w1_z[at : at + 384], "c", SWAP) for at in (0, 384)]
    w2_z = lax.ppermute(w2_in, "zb", SWAP)
    w2_all = [w2, lax.ppermute(w2_in, "c", SWAP), w2_z, lax.ppermute(w2_z, "c", SWAP)]

    flops = 2 * 320 * 3072 * 768
    scratch = [pltpu.VMEM((320, 768), F32)]
    (part,) = kernel_call(first_kernel, [(4, 80, 768)], 7, flops, 8 << 20, scratch, 50)(here, other, *w1_all)
    part = lax.all_to_all(part, "zq", 0, 0, tiled=True)
    (h,) = kernel_call(middle_kernel, [(80, 768)], 2, 20 * 80 * 768, 1 << 20)(part, b1.reshape(1, 768))
    hidden = lax.all_gather(h, "zq", axis=0, tiled=False)
    shapes = [(16, 40, 768)] * 2
    here, other = kernel_call(second_kernel, shapes, 5, flops, 8 << 20, (), 12)(hidden, *w2_all)

    other = lax.all_to_all(other, PLANE, 0, 0, tiled=True)
    here, _ = barrier((here, other))
    here = lax.all_to_all(here, PLANE, 0, 0, tiled=True)
    total = b2.astype(F32)
    for k, out in ((1, other), (0, here)):
        out = out.astype(F32).sum(axis=0).astype(BF16)
        total = total + lax.ppermute(out, CORNER, corner_pairs(k)).astype(F32)
    return total.astype(BF16)


def solution(mesh):
    fine = Mesh(mesh.devices.reshape(SIZES), ROW + COL)
    in_specs = (P(COL, ROW), P(ROW, COL), P(COL), P(COL, ROW), P(ROW))
    return jax.shard_map(shards, mesh=fine, in_specs=in_specs, out_specs=P(COL, ROW), check_vma=False)
```

```python
import jax
import jax.numpy as jnp
from jax import lax
from jax.experimental import pallas as pl
from jax.experimental.pallas import tpu as pltpu
from jax.sharding import Mesh
from jax.sharding import PartitionSpec as P

ROW = ("zq", "zb", "c")
COL = ("yp", "y0", "xp", "x0", "zh")
SIZES = (4, 2, 2, 2, 2, 2, 2, 2)
PLANE = ("yp", "y0", "xp", "x0")
CORNER = ("zb", "c", "y0", "x0", "zh")
SWAP = [(0, 1), (1, 0)]
VMEM = pl.BlockSpec(memory_space=pltpu.VMEM)

F32 = jnp.float32
BF16 = jnp.bfloat16
barrier = lax.optimization_barrier


def corner_pairs(other_zh, with_zb):
    pairs = []
    for i in range(32):
        zb, c, y0, x0, zh = i >> 4, (i >> 3) & 1, (i >> 2) & 1, (i >> 1) & 1, i & 1
        if with_zb:
            zb, y0 = y0, zb
        pairs.append((i, zb << 4 | x0 << 3 | y0 << 2 | c << 1 | (zh ^ other_zh)))
    return pairs


def slot(block, dz, dc):
    y0 = jnp.bitwise_xor(lax.axis_index("zb"), dz)
    x0 = jnp.bitwise_xor(lax.axis_index("c"), dc)
    return (block & 2) * 4 + y0 * 4 + (block & 1) * 2 + x0


def kernel_call(kernel, shapes, n_in, flops, nbytes, scratch=(), limit=12):
    return pl.pallas_call(
        kernel,
        out_shape=[jax.ShapeDtypeStruct(shape, BF16) for shape in shapes],
        in_specs=[VMEM] * n_in,
        out_specs=[VMEM] * len(shapes),
        scratch_shapes=scratch,
        compiler_params=pltpu.CompilerParams(vmem_limit_bytes=limit << 20),
        cost_estimate=pl.CostEstimate(flops=flops, bytes_accessed=nbytes, transcendentals=0),
    )


def spread_kernel(block, out):
    for i in range(16):
        out[i] = block[...]


def first_kernel(got, w0, w1, keep, send):
    zb, c = lax.axis_index("zb"), lax.axis_index("c")
    for out, dy in ((keep, 0), (send, 1)):
        y0 = jnp.bitwise_xor(zb, dy)
        total = None
        for dc, w in enumerate((w0, w1)):
            x0 = jnp.bitwise_xor(c, dc)
            rows = [got[(b & 2) * 4 + y0 * 4 + (b & 1) * 2 + x0] for b in range(4)]
            product = jnp.dot(jnp.concatenate(rows, axis=0), w[...], preferred_element_type=F32)
            total = product if total is None else total + product
        out[...] = total.astype(BF16).reshape(4, 40, 768)


def pair_kernel(here, here_z, other, other_z, part):
    part[:, :40] = (here[...].astype(F32) + here_z[...].astype(F32)).astype(BF16)
    part[:, 40:] = (other[...].astype(F32) + other_z[...].astype(F32)).astype(BF16)


def middle_kernel(parts, bias, h):
    preact = bias[...].astype(F32)
    for k in range(4):
        preact = preact + parts[k].astype(F32)
    h[...] = jax.nn.gelu(preact, approximate=True).astype(BF16)


def second_kernel(hidden, w00, w01, w10, w11, here, other):
    for half, out in ((1, other), (0, here)):
        left = jnp.concatenate([hidden[b, half * 40 : (half + 1) * 40] for b in range(4)], axis=0)
        for k, w in enumerate((w00, w01, w10, w11)):
            product = jnp.dot(left, w[...], preferred_element_type=F32).astype(BF16)
            for b in range(4):
                out[slot(b, k // 2, k % 2)] = product[b * 40 : (b + 1) * 40]


def shards(tokens, w1, b1, w2, b2):
    here, other = (lax.ppermute(tokens, CORNER, corner_pairs(k, False)) for k in range(2))
    w2_in, here = barrier((w2, here))

    shape = [(16, 40, 768)]
    (here,) = kernel_call(spread_kernel, shape, 1, 10**9, 1 << 20)(here)
    (other,) = kernel_call(spread_kernel, shape, 1, 40 * 10**9, 1 << 20)(other)
    here = lax.all_to_all(here, PLANE, 0, 0, tiled=True)
    w1_late, _ = barrier((w1, other))
    w1_c = lax.ppermute(w1_late, "c", SWAP)
    other, _ = barrier((other, here))
    other = lax.all_to_all(other, PLANE, 0, 0, tiled=True)

    w2_z = lax.ppermute(w2_in, "zb", SWAP)
    w2_all = [w2, lax.ppermute(w2_in, "c", SWAP), w2_z, lax.ppermute(w2_z, "c", SWAP)]

    flops = 2 * 320 * 3072 * 768
    first = kernel_call(first_kernel, [(4, 40, 768)] * 2, 3, flops // 2, 4 << 20, (), 50)
    here, _ = barrier((here, w2_z))
    here, send = first(here, w1, w1_c)
    send, _ = barrier((send, w2_z))
    here_z = lax.ppermute(send, "zb", SWAP)
    other, _ = barrier((other, here_z))
    other, send = first(other, w1, w1_c)
    other_z = lax.ppermute(send, "zb", SWAP)
    pair = kernel_call(pair_kernel, [(4, 80, 768)], 4, 10**6, 1 << 20)
    (part,) = pair(here, here_z, other, other_z)
    part = lax.all_to_all(part, "zq", 0, 0, tiled=True)
    (h,) = kernel_call(middle_kernel, [(80, 768)], 2, 20 * 80 * 768, 1 << 20)(part, b1.reshape(1, 768))
    hidden = lax.all_gather(h, "zq", axis=0, tiled=False)
    shapes = [(16, 40, 768)] * 2
    here, other = kernel_call(second_kernel, shapes, 5, flops, 8 << 20, (), 12)(hidden, *w2_all)

    other = lax.all_to_all(other, PLANE, 0, 0, tiled=True)
    here, _ = barrier((here, other))
    here = lax.all_to_all(here, PLANE, 0, 0, tiled=True)
    total = b2.astype(F32)
    for k, out in ((1, other), (0, here)):
        out = out.astype(F32).sum(axis=0).astype(BF16)
        total = total + lax.ppermute(out, CORNER, corner_pairs(k, True)).astype(F32)
    return total.astype(BF16)


def solution(mesh):
    fine = Mesh(mesh.devices.reshape(SIZES), ROW + COL)
    in_specs = (P(COL, ROW), P(ROW, COL), P(COL), P(COL, ROW), P(ROW))
    return jax.shard_map(shards, mesh=fine, in_specs=in_specs, out_specs=P(COL, ROW), check_vma=False)
```
